32 devices in a mesh: det: 4 (over z), src: 8 (over y, x, core).
Axes of the slice: x: 2, y: 2, z: 4, core: 2. Of those that a mesh axis runs over, the one named last changes fastest.
Arguments:
- patches: bfloat16 [2048, 2, 128, 128], P(('det', 'src')), may hold values from -0.046875 to 0.046875
- owners: int32 [2048, 2], P(('det', 'src')), may hold values from 0 to 7, all different within a row; in each aligned block of 64 rows (0 to 63, 64 to 127, ...) at most 32 rows name the same one
- tap_weights: float32 [8, 2, 31], P('src'), may hold values from -0.1 to 1.2
Outputs:
- gram_self: float32 [2048, 512], P(('det', 'src'))
- gram_cross: float32 [2048, 512], P(('det', 'src'))
The draws below stay inside these ranges and needn't reach their ends.
Inputs may be any that keep to these rules, and one draw needn't show every extreme that they name: `owners`: each row names 2 different source blocks. Among the 64 detectors of one device (aligned blocks of rows) no block is named more than 32 times, and in every draw some device names some block exactly 32 times.
All inputs are finite; a program needn't handle non-finite values.
Results may differ from the reference program's by a relative error of at most 0.0093.
Values may be sent and summed in bfloat16 or wider, within the bound.
A program may use at most 128 MiB of HBM per device.

```python
import math
import jax
import jax.numpy as jnp
import numpy as np
from jax import lax

BLK = 128
TAPS = 31
TOUCH = 2
DET_DEV = 64
DETP = 512
DETECTORS = 2048
CAP = 32
SLOTS = 256
N_DET = 4
N_SRC = 8


def draw_tap_weights(key, part):
    key = jax.random.fold_in(key, 11)
    size_key, flip_key, middle_key = jax.random.split(key, 3)
    shape_all = (N_SRC, 2, TAPS)
    size_taps = jnp.exp(jax.random.uniform(size_key, shape_all, jnp.float32, math.log(0.01), math.log(0.1)))
    middle = jnp.exp(jax.random.uniform(middle_key, (N_SRC, 2, 1), jnp.float32, math.log(0.8), math.log(1.2)))
    sign_flip = (2 * jax.random.randint(flip_key, shape_all, 0, 2) - 1).astype(jnp.float32)
    centre = jnp.arange(TAPS, dtype=jnp.int32) == TAPS // 2
    return jnp.where(centre[None, None, :], middle, size_taps * sign_flip).astype(jnp.float32)


def shard_levels(rng, shape, cuts, low, high):
    def one(axis_at, blocks):
        steps = jax.random.uniform(jax.random.fold_in(jax.random.fold_in(rng, 6), axis_at), (blocks,), jnp.float32, low / len(cuts), high / len(cuts))
        return jnp.repeat(jnp.exp(steps), shape[axis_at] // blocks).reshape((-1,) + (1,) * (len(shape) - axis_at - 1))

    gain = one(*cuts[0])
    for cut in cuts[1:]:
        gain = gain * one(*cut)
    return gain


def deal_out(rng, own, number, rows, count, top, reach, slope):
    order = jax.random.permutation(rng, count)
    packed, common = load_shares(count, rows * top, reach, slope, True), load_shares(count, rows * top, reach, slope, False)
    places = jnp.arange(count)

    def named(sizes, rotation):
        used = int((sizes > 0).sum())
        fixed = max(1, used // 4)
        passed = fixed + (places - fixed + rotation * (used - fixed)) % max(1, count - fixed)
        return jnp.zeros((count,), jnp.int32).at[order[jnp.where(places < fixed, places, passed)]].set(jnp.asarray(sizes, jnp.int32))

    sizes = jnp.where(number % 4 == 0, named(packed, number // 4), named(common, number - number // 4 - 1))
    mixed = jax.random.permutation(jax.random.fold_in(own, 3), count)
    giver, taker = mixed[0:count // 2 * 2:2], mixed[1:count // 2 * 2:2]
    margin = jnp.minimum(sizes[giver] - 1, reach - sizes[taker]) // 2
    margin = jnp.where((giver == order[0]) | (taker == order[0]) | (sizes[taker] == 0), 0, jnp.maximum(margin, 0))
    passed = jax.random.randint(jax.random.fold_in(own, 4), (count // 2,), 0, 1 << 20) % (margin + 1)
    sizes = sizes.at[giver].add(-passed).at[taker].add(passed)
    labels = jnp.searchsorted(jnp.cumsum(sizes), jnp.arange(rows * top), side="right").astype(jnp.int32)
    table = labels.reshape(top, rows).T
    table = table[jax.random.permutation(jax.random.fold_in(own, 1), rows)]
    rotation = jax.random.randint(jax.random.fold_in(own, 2), (rows, 1), 0, top)
    return jnp.take_along_axis(table, (jnp.arange(top)[None, :] + rotation) % top, axis=1)


def load_shares(number_of, total, most, slope, full):
    portions = [(1 << 20) // math.isqrt(grade ** slope) + 1 for grade in range(1, number_of + 1)]
    largest = most if full else min(most, max(-(-total // number_of), total * portions[0] // sum(portions)))
    least = 1 if total - largest >= number_of - 1 else 0
    given, surplus = [largest] + [least] * (number_of - 1), total - largest - least * (number_of - 1)
    while surplus > 0:
        movable = [i for i in range(1, number_of) if given[i] < largest] or [i for i in range(1, number_of) if given[i] < most]
        pool, remaining = sum([portions[i] for i in movable]), surplus
        for i in movable:
            more = min(most - given[i], max(1, remaining * portions[i] // pool), surplus)
            given[i] = given[i] + more
            surplus = surplus - more
    return np.array(given)


def normal_values(own_key, shape, deviation, most, shards=(), kind=jnp.bfloat16):
    drawn = jax.random.normal(own_key, shape, jnp.float32) * deviation
    if len(shards) > 0:
        drawn = shard_levels(own_key, shape, shards, -0.22, 0.18) * drawn
    return jnp.clip(drawn, min=-most, max=most).astype(kind)


def setup_inputs(seed: int = 0) -> dict:
    key_of = jax.random.split(jax.random.key(seed), 4)
    patches = normal_values(key_of[0], (DETECTORS, TOUCH, BLK, BLK), (1.0 / BLK), 0.046875, ((0, 32),))
    owners_keys = jax.random.split(jax.random.fold_in(key_of[1], 1), DETECTORS // DET_DEV)
    owners_turns = jax.random.permutation(jax.random.fold_in(key_of[1], 3), DETECTORS // DET_DEV)
    owners = jax.vmap(lambda own, number: deal_out(jax.random.fold_in(key_of[1], 2), own, number, DET_DEV, N_SRC, TOUCH, CAP, 2))(owners_keys, owners_turns).reshape((DETECTORS, TOUCH))
    tap_weights = draw_tap_weights(jax.random.fold_in(key_of[3], 71), 0)
    return dict(patches=patches, owners=owners, tap_weights=tap_weights)


def make_bands(tap_weights):
    offset = jnp.arange(BLK, dtype=jnp.int32)[None, :] - jnp.arange(BLK, dtype=jnp.int32)[:, None] + TAPS // 2
    inside = (offset >= 0) & (offset < TAPS)
    position = jnp.clip(offset, 0, TAPS - 1)
    return jnp.where(inside, tap_weights[..., position], jnp.zeros((), jnp.float32)).astype(jnp.bfloat16)


def smooth_panel(pieces, owner_ids, band_mats):
    col_band = jnp.take(band_mats[:, 0], owner_ids, axis=0).astype(jnp.float32)
    row_band = jnp.take(band_mats[:, 1], owner_ids, axis=0).astype(jnp.float32)
    half_done = jnp.einsum("nic,nrc->nir", pieces.astype(jnp.float32), col_band, precision=lax.Precision.HIGHEST).astype(jnp.bfloat16)
    return jnp.einsum("nki,nij->nkj", row_band, half_done.astype(jnp.float32), precision=lax.Precision.HIGHEST).astype(jnp.bfloat16)


def owner_groups(owner_row):
    ordering = jnp.argsort(owner_row, stable=True).astype(jnp.int32)
    counts = jnp.sum((owner_row[None, :] == jnp.arange(N_SRC, dtype=jnp.int32)[:, None]).astype(jnp.int32), axis=1)
    starts = (jnp.cumsum(counts) - counts).astype(jnp.int32)
    padded = jnp.concatenate([ordering, jnp.zeros((SLOTS,), jnp.int32)])
    return padded, counts, starts


def group_rows(flat_rows, padded, counts, starts, owner_id):
    picked = lax.dynamic_slice(padded, (starts[owner_id],), (SLOTS,))
    live_rows = jnp.arange(SLOTS, dtype=jnp.int32) < counts[owner_id]
    group = jnp.where(live_rows[:, None], jnp.take(flat_rows, picked, axis=0), jnp.zeros((), jnp.bfloat16))
    return group, (picked // TOUCH).astype(jnp.int32)


def reference(patches, owners, tap_weights):
    band_mats = make_bands(tap_weights)
    records = DETP * TOUCH
    pieces = patches.reshape(N_DET, records, BLK, BLK)
    owner_rows = owners.reshape(N_DET, records)
    smoothed = lax.map(lambda pair_args: smooth_panel(pair_args[0], pair_args[1], band_mats), (pieces, owner_rows))
    flat_rows = smoothed.reshape(N_DET, records, BLK * BLK)
    padded, counts, starts = jax.vmap(owner_groups)(owner_rows)

    def panel_gram(panel_id):
        other_id = (panel_id + N_DET // 2) % N_DET

        def add_owner(totals_in, owner_id):
            own_group, own_det = group_rows(flat_rows[panel_id], padded[panel_id], counts[panel_id], starts[panel_id], owner_id)
            theirs, their_det = group_rows(flat_rows[other_id], padded[other_id], counts[other_id], starts[other_id], owner_id)
            gram_mine = jnp.dot(own_group, own_group.T, preferred_element_type=jnp.float32)
            gram_other = jnp.dot(own_group, theirs.T, preferred_element_type=jnp.float32)
            self_sum = totals_in[0].at[own_det[:, None], own_det[None, :]].add(gram_mine)
            cross_sum = totals_in[1].at[own_det[:, None], their_det[None, :]].add(gram_other)
            return (self_sum, cross_sum), None

        empty = jnp.zeros((DETP, DETP), jnp.float32)
        totals = lax.scan(add_owner, (empty, empty), jnp.arange(N_SRC, dtype=jnp.int32))[0]
        return totals

    gram_self, gram_cross = lax.map(panel_gram, jnp.arange(N_DET, dtype=jnp.int32))
    return gram_self.reshape(N_DET * DETP, DETP), gram_cross.reshape(N_DET * DETP, DETP)
```

```python
import functools

import jax
import jax.numpy as jnp
from jax import lax
from jax.experimental import pallas as pl
from jax.experimental.pallas import tpu as pltpu
from jax.sharding import PartitionSpec as P


def make_bands(taps, edge):
    count = taps.shape[-1]
    place = jnp.arange(edge, dtype=jnp.int32)
    offset = place[None, :] - place[:, None] + count // 2
    table = (offset[None] == jnp.arange(count, dtype=jnp.int32)[:, None, None]).astype(jnp.float32)
    return jnp.einsum("...t,tij->...ij", taps, table, precision=lax.Precision.HIGHEST).astype(
        jnp.bfloat16
    )


def smooth_kernel(owner_ref, patch_ref, band_ref, out_ref):
    touch, rows = out_ref.shape[0], out_ref.shape[1]
    base = pl.program_id(0) * rows

    for i in range(rows):
        for t in range(touch):
            own = owner_ref[base + i, t]
            half = lax.dot_general(
                patch_ref[i, t],
                band_ref[own, 0],
                (((1,), (1,)), ((), ())),
                preferred_element_type=jnp.float32,
            ).astype(jnp.bfloat16)
            out_ref[t, i] = jnp.dot(
                band_ref[own, 1], half, preferred_element_type=jnp.float32
            ).astype(jnp.bfloat16)


def smooth(patches, owners, bands):
    det, touch, edge, _ = patches.shape
    step = 8
    return pl.pallas_call(
        smooth_kernel,
        grid_spec=pltpu.PrefetchScalarGridSpec(
            num_scalar_prefetch=1,
            grid=(det // step,),
            in_specs=[
                pl.BlockSpec((step, touch, edge, edge), lambda g, o: (g, 0, 0, 0)),
                pl.BlockSpec(bands.shape, lambda g, o: (0, 0, 0, 0)),
            ],
            out_specs=pl.BlockSpec((touch, step, edge, edge), lambda g, o: (0, g, 0, 0)),
        ),
        out_shape=jax.ShapeDtypeStruct((touch, det, edge, edge), jnp.bfloat16),
        compiler_params=pltpu.CompilerParams(vmem_limit_bytes=32 << 20),
    )(owners, patches, bands)


def gram_kernel(left_ref, right_ref, left_own_ref, right_own_ref, out_ref):
    touch = left_ref.shape[0]
    total = None
    for t in range(touch):
        for u in range(touch):
            part = lax.dot_general(
                left_ref[t],
                right_ref[u],
                (((1,), (1,)), ((), ())),
                preferred_element_type=jnp.float32,
            )
            same = left_own_ref[:, t : t + 1] == right_own_ref[u : u + 1, :]
            part = jnp.where(same, part, 0.0)
            total = part if total is None else total + part
    out_ref[...] = total.astype(jnp.bfloat16)


def gram(left, right, left_own, right_own):
    touch, count, depth = right.shape
    block = 256
    return pl.pallas_call(
        gram_kernel,
        grid=(count // block, count // block),
        in_specs=[
            pl.BlockSpec((touch, block, depth), lambda i, j: (0, i, 0)),
            pl.BlockSpec((touch, block, depth), lambda i, j: (0, j, 0)),
            pl.BlockSpec((block, touch), lambda i, j: (i, 0)),
            pl.BlockSpec((touch, block), lambda i, j: (0, j)),
        ],
        out_specs=pl.BlockSpec((block, block), lambda i, j: (i, j)),
        out_shape=jax.ShapeDtypeStruct((count, count), jnp.bfloat16),
        compiler_params=pltpu.CompilerParams(vmem_limit_bytes=32 << 20),
        cost_estimate=pl.CostEstimate(
            flops=2 * touch * touch * count * count * depth,
            bytes_accessed=4 * touch * count * depth,
            transcendentals=0,
        ),
    )(left, right, left_own, right_own.T)


def share(parts, src):
    rows = parts.shape[0] // src
    got = lax.all_to_all(parts, "src", split_axis=0, concat_axis=0, tiled=True)
    return jnp.sum(got.reshape(src, rows, -1).astype(jnp.float32), axis=0)


def on_device(patches, owners, tap_weights):
    src = lax.axis_size("src")
    det_axis = lax.axis_size("det")
    det, touch, edge, _ = patches.shape
    cells = edge * edge
    swap = [(i, (i + det_axis // 2) % det_axis) for i in range(det_axis)]
    taps = lax.all_gather(tap_weights, "src", axis=0, tiled=True)
    panel_own = lax.all_gather(owners, "src", axis=0, tiled=True)
    other_own = lax.ppermute(panel_own, "det", swap)
    bands = make_bands(taps, edge)
    smoothed = smooth(patches, owners, bands).reshape(touch, det, cells)
    upper = lax.axis_index("det") >= det_axis // 2
    low, high = smoothed[:, :, : cells // 2], smoothed[:, :, cells // 2 :]
    kept = jnp.where(upper, high, low)
    given = jnp.where(upper, low, high)
    other = lax.ppermute(given, "det", swap)
    chunks = jnp.stack([kept.reshape(touch, det, src, -1), given.reshape(touch, det, src, -1)], 3)
    mine = lax.all_to_all(
        chunks.reshape(touch, det, cells), "src", split_axis=2, concat_axis=1, tiled=True
    )
    self_part = gram(mine, mine, panel_own, panel_own)
    result_self = share(self_part, src)
    theirs = lax.all_to_all(other, "src", split_axis=2, concat_axis=1, tiled=True)
    cross = gram(mine, theirs, panel_own, other_own)
    rows = share(cross, src)
    columns = share(cross.T, src)
    result_cross = rows + lax.ppermute(columns.astype(jnp.bfloat16), "det", swap).astype(
        jnp.float32
    )
    return result_self, result_cross


def solution(mesh):
    return jax.shard_map(
        on_device,
        mesh=mesh,
        in_specs=(
            P(("det", "src"), None, None, None),
            P(("det", "src"), None),
            P("src", None, None),
        ),
        out_specs=(P(("det", "src"), None), P(("det", "src"), None)),
        check_vma=False,
    )
```

```python
import functools

import jax
import jax.numpy as jnp
from jax import lax
from jax.experimental import pallas as pl
from jax.experimental.pallas import tpu as pltpu
from jax.sharding import PartitionSpec as P

MESH = pl.DeviceIdType.MESH


def make_bands(taps, edge):
    count = taps.shape[-1]
    place = jnp.arange(edge, dtype=jnp.int32)
    offset = place[None, :] - place[:, None] + count // 2
    table = (offset[None] == jnp.arange(count, dtype=jnp.int32)[:, None, None]).astype(jnp.float32)
    return jnp.einsum("...t,tij->...ij", taps, table, precision=lax.Precision.HIGHEST).astype(
        jnp.bfloat16
    )


def smooth_kernel(owner_ref, patch_ref, band_ref, out_ref, spread_ref):
    rows, edge = patch_ref.shape[0], patch_ref.shape[2]
    t, base = pl.program_id(0), pl.program_id(1) * rows
    for i in range(rows):
        own = owner_ref[base + i, t]
        half = lax.dot_general(
            patch_ref[i, 0],
            band_ref[own, 0],
            (((1,), (1,)), ((), ())),
            preferred_element_type=jnp.float32,
        ).astype(jnp.bfloat16)
        spread_ref[pl.ds(i, edge, stride=rows), :] = jnp.dot(
            band_ref[own, 1], half, preferred_element_type=jnp.float32
        )
    out_ref[...] = spread_ref[...].reshape(out_ref.shape).astype(jnp.bfloat16)


def smooth(patches, owners, bands):
    det, touch, edge, _ = patches.shape
    step = 16
    steps = det // step
    return pl.pallas_call(
        smooth_kernel,
        grid_spec=pltpu.PrefetchScalarGridSpec(
            num_scalar_prefetch=1,
            grid=(touch, steps),
            in_specs=[
                pl.BlockSpec((step, 1, edge, edge), lambda t, g, o: (g, t, 0, 0)),
                pl.BlockSpec(bands.shape, lambda t, g, o: (0, 0, 0, 0)),
            ],
            out_specs=pl.BlockSpec((edge, step, edge), lambda t, g, o: (0, t * steps + g, 0)),
            scratch_shapes=[pltpu.VMEM((edge * step, edge), jnp.float32)],
        ),
        out_shape=jax.ShapeDtypeStruct((edge, touch * det, edge), jnp.bfloat16),
        compiler_params=pltpu.CompilerParams(vmem_limit_bytes=32 << 20),
    )(owners, patches, bands)


def gram_kernel(
    src, dets, touch, group,
    s_ref, po_ref, pot_ref, oo_ref, oot_ref,
    self_ref, cross_ref,
    mine, theirs, out_a, out_b, in_self, in_row, in_col, col_out, col_in,
    x_send, x_recv, m_send, m_recv, g_send, g_recv, c_sem,
):
    me, pd = lax.axis_index("src"), lax.axis_index("det")
    partner = lax.rem(pd + dets // 2, dets)
    upper, other_upper = pd // (dets // 2), partner // (dets // 2)
    share = mine.shape[1]
    half = share // 2
    det = mine.shape[2] // touch
    panel = src * det

    barrier = pltpu.get_barrier_semaphore()

    @pl.loop(1, src)
    def _(o):
        to = lax.rem(me + o, src)
        pl.semaphore_signal(barrier, inc=1, device_id=(pd, to), device_id_type=MESH)

    @pl.loop(0, src)
    def _(o):
        to = lax.rem(me + o, src)
        pl.semaphore_signal(barrier, inc=1, device_id=(partner, to), device_id_type=MESH)

    pl.semaphore_wait(barrier, 2 * src - 1)

    def cross_copy(o):
        to = lax.rem(me + o, src)
        return pltpu.make_async_remote_copy(
            src_ref=s_ref.at[pl.ds(to * share + other_upper * half, half)],
            dst_ref=theirs.at[me],
            send_sem=x_send.at[o],
            recv_sem=x_recv.at[o],
            device_id=(partner, to),
            device_id_type=MESH,
        )

    def self_copy(o):
        to = lax.rem(me + o, src)
        return pltpu.make_async_remote_copy(
            src_ref=s_ref.at[pl.ds(to * share, share)],
            dst_ref=mine.at[me],
            send_sem=m_send.at[o],
            recv_sem=m_recv.at[o],
            device_id=(pd, to),
            device_id_type=MESH,
        )

    def gram_copy(kind, o, source, target):
        to = lax.rem(me + o, src)
        return pltpu.make_async_remote_copy(
            src_ref=source.at[to],
            dst_ref=target.at[me],
            send_sem=g_send.at[kind, o],
            recv_sem=g_recv.at[kind, o],
            device_id=(pd, to),
            device_id_type=MESH,
        )

    def piece(ref, start, count, first, depth, t):
        return jnp.concatenate(
            [
                ref[pl.ds(start, count), first + k, t * det : (t + 1) * det, :].reshape(
                    count * det, ref.shape[3]
                )
                for k in range(depth)
            ],
            axis=1,
        )

    def partial(left, left_at, left_own, right, right_at, right_own, depth, out):
        @pl.loop(0, src // group)
        def _(g):
            start = pl.multiple_of(g * (group * det), group * det)
            total = None
            for u in range(touch):
                wide = piece(right, 0, src, right_at, depth, u)
                for t in range(touch):
                    part = lax.dot_general(
                        piece(left, g * group, group, left_at, depth, t),
                        wide,
                        (((1,), (1,)), ((), ())),
                        preferred_element_type=jnp.float32,
                    )
                    same = (
                        left_own[pl.ds(start, group * det), t : t + 1] == right_own[u : u + 1, :]
                    )
                    part = jnp.where(same, part, 0.0)
                    total = part if total is None else total + part
            out[pl.ds(g * group, group)] = total.reshape(group, det, panel).astype(jnp.bfloat16)

    def scatter(kind, source, target):
        @pl.loop(1, src)
        def _(o):
            gram_copy(kind, o, source, target).start()

        target[me] = source[me]

    def collect(kind, source, target):
        @pl.loop(1, src)
        def _(o):
            gram_copy(kind, o, source, target).wait_recv()

        total = target[0].astype(jnp.float32)
        for i in range(1, src):
            total = total + target[i].astype(jnp.float32)
        return total

    def sent(kind, source, target):
        @pl.loop(1, src)
        def _(o):
            gram_copy(kind, o, source, target).wait_send()

    @pl.loop(0, src)
    def _(o):
        cross_copy(o).start()

    own = pltpu.make_async_copy(s_ref.at[pl.ds(me * share, share)], mine.at[me], m_send.at[0])
    own.start()

    @pl.loop(1, src)
    def _(o):
        self_copy(o).start()

    own.wait()

    @pl.loop(1, src)
    def _(o):
        self_copy(o).wait()

    partial(mine, 0, po_ref, mine, 0, pot_ref, share, out_a)
    scatter(0, out_a, in_self)
    self_ref[...] = collect(0, out_a, in_self)
    sent(0, out_a, in_self)

    @pl.loop(0, src)
    def _(o):
        cross_copy(o).wait()

    partial(theirs, 0, oo_ref, mine, upper * half, pot_ref, half, out_a)
    scatter(1, out_a, in_col)
    partial(mine, upper * half, po_ref, theirs, 0, oot_ref, half, out_b)
    scatter(2, out_b, in_row)
    col_out[...] = collect(1, out_a, in_col).astype(jnp.bfloat16)
    last = pltpu.make_async_remote_copy(
        src_ref=col_out,
        dst_ref=col_in,
        send_sem=c_sem.at[0],
        recv_sem=c_sem.at[1],
        device_id=(partner, me),
        device_id_type=MESH,
    )
    last.start()
    rows = collect(2, out_b, in_row)
    sent(1, out_a, in_col)
    sent(2, out_b, in_row)
    last.wait()
    cross_ref[...] = rows + col_in[...].astype(jnp.float32)


def on_device(patches, owners, tap_weights):
    src = lax.axis_size("src")
    dets = lax.axis_size("det")
    det, touch, edge, _ = patches.shape
    panel = det * src
    share = edge // src
    swap = [(i, (i + dets // 2) % dets) for i in range(dets)]
    taps = lax.all_gather(tap_weights, "src", axis=0, tiled=True)
    panel_own = lax.all_gather(owners, "src", axis=0, tiled=True)
    other_own = lax.ppermute(panel_own, "det", swap)
    bands = make_bands(taps, edge)
    smoothed = smooth(patches, owners, bands)
    vmem = pl.BlockSpec(memory_space=pltpu.VMEM)
    dma = pltpu.SemaphoreType.DMA
    block = pltpu.VMEM((src, det, panel), jnp.bfloat16)
    line = pltpu.VMEM((det, panel), jnp.bfloat16)
    return pl.pallas_call(
        functools.partial(gram_kernel, src, dets, touch, min(src, 4)),
        out_shape=[jax.ShapeDtypeStruct((det, panel), jnp.float32)] * 2,
        in_specs=[pl.BlockSpec(memory_space=pl.ANY)] + [vmem] * 4,
        out_specs=[vmem] * 2,
        scratch_shapes=[
            pltpu.VMEM((src, share, touch * det, edge), jnp.bfloat16),
            pltpu.VMEM((src, share // 2, touch * det, edge), jnp.bfloat16),
            block, block, block, block, block, line, line,
            dma((src,)), dma((src,)), dma((src,)), dma((src,)),
            dma((3, src)), dma((3, src)), dma((2,)),
        ],
        compiler_params=pltpu.CompilerParams(
            collective_id=0, has_side_effects=True, vmem_limit_bytes=60 << 20
        ),
        cost_estimate=pl.CostEstimate(
            flops=8 * panel * panel * share * edge * 2,
            bytes_accessed=4 * det * touch * edge * edge,
            transcendentals=0,
        ),
    )(smoothed, panel_own, panel_own.T, other_own, other_own.T)


def solution(mesh):
    return jax.shard_map(
        on_device,
        mesh=mesh,
        in_specs=(
            P(("det", "src"), None, None, None),
            P(("det", "src"), None),
            P("src", None, None),
        ),
        out_specs=(P(("det", "src"), None), P(("det", "src"), None)),
        check_vma=False,
    )
```

```python
import functools

import jax
import jax.numpy as jnp
from jax import lax
from jax.experimental import pallas as pl
from jax.experimental.pallas import tpu as pltpu
from jax.sharding import PartitionSpec as P

MESH = pl.DeviceIdType.MESH


def make_bands(taps, edge):
    count = taps.shape[-1]
    place = jnp.arange(edge, dtype=jnp.int32)
    offset = place[None, :] - place[:, None] + count // 2
    table = (offset[None] == jnp.arange(count, dtype=jnp.int32)[:, None, None]).astype(jnp.float32)
    return jnp.einsum("...t,tij->...ij", taps, table, precision=lax.Precision.HIGHEST).astype(
        jnp.bfloat16
    )


def spread_kernel(
    src, dets, own_ref, tap_ref, mine_ref, other_ref, taps_ref,
    mine, other, taps, m_send, m_recv, o_send, o_recv, t_send, t_recv,
):
    me, pd = lax.axis_index("src"), lax.axis_index("det")
    partner = lax.rem(pd + dets // 2, dets)
    barrier = pltpu.get_barrier_semaphore()

    @pl.loop(1, src)
    def _(o):
        to = lax.rem(me + o, src)
        pl.semaphore_signal(barrier, inc=1, device_id=(pd, to), device_id_type=MESH)

    @pl.loop(0, src)
    def _(o):
        to = lax.rem(me + o, src)
        pl.semaphore_signal(barrier, inc=1, device_id=(partner, to), device_id_type=MESH)

    pl.semaphore_wait(barrier, 2 * src - 1)

    def copy(o, source, target, send, recv, panel):
        return pltpu.make_async_remote_copy(
            src_ref=source,
            dst_ref=target.at[me],
            send_sem=send.at[o],
            recv_sem=recv.at[o],
            device_id=(panel, lax.rem(me + o, src)),
            device_id_type=MESH,
        )

    @pl.loop(1, src)
    def _(o):
        copy(o, tap_ref, taps, t_send, t_recv, pd).start()
        copy(o, own_ref, mine, m_send, m_recv, pd).start()

    @pl.loop(0, src)
    def _(o):
        copy(o, own_ref, other, o_send, o_recv, partner).start()

    taps[me] = tap_ref[...]
    mine[me] = own_ref[...]

    @pl.loop(1, src)
    def _(o):
        copy(o, tap_ref, taps, t_send, t_recv, pd).wait()
        copy(o, own_ref, mine, m_send, m_recv, pd).wait()

    @pl.loop(0, src)
    def _(o):
        copy(o, own_ref, other, o_send, o_recv, partner).wait()

    taps_ref[...] = taps[...]
    mine_ref[...] = mine[...]
    other_ref[...] = other[...]


def spread(owners, tap_weights, src, dets):
    vmem = pl.BlockSpec(memory_space=pltpu.VMEM)
    own = (src, *owners.shape)
    tap = (src, *tap_weights.shape)
    return pl.pallas_call(
        functools.partial(spread_kernel, src, dets),
        out_shape=[
            jax.ShapeDtypeStruct(own, jnp.int32),
            jax.ShapeDtypeStruct(own, jnp.int32),
            jax.ShapeDtypeStruct(tap, jnp.float32),
        ],
        in_specs=[vmem] * 2,
        out_specs=[vmem] * 3,
        scratch_shapes=[
            pltpu.VMEM(own, jnp.int32), pltpu.VMEM(own, jnp.int32), pltpu.VMEM(tap, jnp.float32),
        ] + [pltpu.SemaphoreType.DMA((src,))] * 6,
        compiler_params=pltpu.CompilerParams(
            collective_id=1, has_side_effects=True, vmem_limit_bytes=16 << 20
        ),
    )(owners, tap_weights)


def gram_kernel(
    src, dets, touch, group, step,
    owner_ref, patch_ref, band_ref, po_ref, pot_ref, oo_ref, oot_ref,
    self_ref, cross_ref,
    s_ref, spread_ref, mine, theirs, out_a, out_b, in_self, in_row, in_col, col_out, col_in,
    x_send, x_recv, m_send, m_recv, g_send, g_recv, c_sem,
):
    me, pd = lax.axis_index("src"), lax.axis_index("det")
    partner = lax.rem(pd + dets // 2, dets)
    upper, other_upper = pd // (dets // 2), partner // (dets // 2)
    share = mine.shape[1]
    half = share // 2
    det = mine.shape[2] // touch
    panel = src * det

    barrier = pltpu.get_barrier_semaphore()

    @pl.loop(1, src)
    def _(o):
        to = lax.rem(me + o, src)
        pl.semaphore_signal(barrier, inc=1, device_id=(pd, to), device_id_type=MESH)

    @pl.loop(0, src)
    def _(o):
        to = lax.rem(me + o, src)
        pl.semaphore_signal(barrier, inc=1, device_id=(partner, to), device_id_type=MESH)

    pl.semaphore_wait(barrier, 2 * src - 1)

    def cross_copy(o, first=0, count=touch * det):
        to = lax.rem(me + o, src)
        records = pl.ds(first, count)
        return pltpu.make_async_remote_copy(
            src_ref=s_ref.at[pl.ds(to * share + other_upper * half, half), records],
            dst_ref=theirs.at[me, :, records],
            send_sem=x_send.at[o],
            recv_sem=x_recv.at[o],
            device_id=(partner, to),
            device_id_type=MESH,
        )

    def self_copy(o, first=0, count=touch * det):
        to = lax.rem(me + o, src)
        records = pl.ds(first, count)
        return pltpu.make_async_remote_copy(
            src_ref=s_ref.at[pl.ds(to * share, share), records],
            dst_ref=mine.at[me, :, records],
            send_sem=m_send.at[o],
            recv_sem=m_recv.at[o],
            device_id=(pd, to),
            device_id_type=MESH,
        )

    def gram_copy(kind, o, source, target):
        to = lax.rem(me + o, src)
        return pltpu.make_async_remote_copy(
            src_ref=source.at[to],
            dst_ref=target.at[me],
            send_sem=g_send.at[kind, o],
            recv_sem=g_recv.at[kind, o],
            device_id=(pd, to),
            device_id_type=MESH,
        )

    def piece(ref, start, count, first, depth, t):
        return jnp.concatenate(
            [
                ref[pl.ds(start, count), first + k, t * det : (t + 1) * det, :].reshape(
                    count * det, ref.shape[3]
                )
                for k in range(depth)
            ],
            axis=1,
        )

    def partial(left, left_at, left_own, right, right_at, right_own, depth, out):
        @pl.loop(0, src // group)
        def _(g):
            start = pl.multiple_of(g * (group * det), group * det)
            total = None
            for u in range(touch):
                wide = piece(right, 0, src, right_at, depth, u)
                for t in range(touch):
                    part = lax.dot_general(
                        piece(left, g * group, group, left_at, depth, t),
                        wide,
                        (((1,), (1,)), ((), ())),
                        preferred_element_type=jnp.float32,
                    )
                    same = (
                        left_own[pl.ds(start, group * det), t : t + 1] == right_own[u : u + 1, :]
                    )
                    part = jnp.where(same, part, 0.0)
                    total = part if total is None else total + part
            out[pl.ds(g * group, group)] = total.reshape(group, det, panel).astype(jnp.bfloat16)

    def scatter(kind, source, target):
        @pl.loop(1, src)
        def _(o):
            gram_copy(kind, o, source, target).start()

        target[me] = source[me]

    def collect(kind, source, target):
        @pl.loop(1, src)
        def _(o):
            gram_copy(kind, o, source, target).wait_recv()

        total = target[0].astype(jnp.float32)
        for i in range(1, src):
            total = total + target[i].astype(jnp.float32)
        return total

    def sent(kind, source, target):
        @pl.loop(1, src)
        def _(o):
            gram_copy(kind, o, source, target).wait_send()

    edge = patch_ref.shape[2]
    steps = det // step

    @pl.loop(0, touch * steps)
    def _(q):
        t, base = q // steps, lax.rem(q, steps) * step
        for i in range(step):
            named = owner_ref[base + i, t]
            middle = lax.dot_general(
                patch_ref[base + i, t],
                band_ref[named, 0],
                (((1,), (1,)), ((), ())),
                preferred_element_type=jnp.float32,
            ).astype(jnp.bfloat16)
            spread_ref[pl.ds(i, edge, stride=step), :] = jnp.dot(
                band_ref[named, 1], middle, preferred_element_type=jnp.float32
            )
        first = pl.multiple_of(q * step, step)
        s_ref[:, pl.ds(first, step), :] = (
            spread_ref[...].reshape(edge, step, edge).astype(jnp.bfloat16)
        )

        @pl.loop(0, src)
        def _(o):
            cross_copy(o, first, step).start()

        @pl.when(lax.rem(q, steps) == steps - 1)
        def _():
            @pl.loop(1, src)
            def _(o):
                self_copy(o, pl.multiple_of(t * det, det), det).start()

    own = pltpu.make_async_copy(s_ref.at[pl.ds(me * share, share)], mine.at[me], m_send.at[0])
    own.start()
    own.wait()

    @pl.loop(1, src)
    def _(o):
        self_copy(o).wait()

    partial(mine, 0, po_ref, mine, 0, pot_ref, share, out_a)
    scatter(0, out_a, in_self)
    self_ref[...] = collect(0, out_a, in_self)
    sent(0, out_a, in_self)

    @pl.loop(0, src)
    def _(o):
        cross_copy(o).wait()

    partial(theirs, 0, oo_ref, mine, upper * half, pot_ref, half, out_a)
    scatter(1, out_a, in_col)
    single = out_b.shape[0] < src
    if single:
        sent(1, out_a, in_col)
        out_b = out_a
    partial(mine, upper * half, po_ref, theirs, 0, oot_ref, half, out_b)
    scatter(2, out_b, in_row)
    col_out[...] = collect(1, out_a, in_col).astype(jnp.bfloat16)
    last = pltpu.make_async_remote_copy(
        src_ref=col_out,
        dst_ref=col_in,
        send_sem=c_sem.at[0],
        recv_sem=c_sem.at[1],
        device_id=(partner, me),
        device_id_type=MESH,
    )
    last.start()
    rows = collect(2, out_b, in_row)
    if not single:
        sent(1, out_a, in_col)
    sent(2, out_b, in_row)
    last.wait()
    cross_ref[...] = rows + col_in[...].astype(jnp.float32)


def on_device(patches, owners, tap_weights):
    src = lax.axis_size("src")
    dets = lax.axis_size("det")
    det, touch, edge, _ = patches.shape
    panel = det * src
    share = edge // src
    panel_own, other_own, taps = spread(owners, tap_weights, src, dets)
    panel_own = panel_own.reshape(panel, touch)
    other_own = other_own.reshape(panel, touch)
    bands = make_bands(taps.reshape(src, 2, -1), edge)
    vmem = pl.BlockSpec(memory_space=pltpu.VMEM)
    dma = pltpu.SemaphoreType.DMA
    block = pltpu.VMEM((src, det, panel), jnp.bfloat16)
    line = pltpu.VMEM((det, panel), jnp.bfloat16)
    second = block if panel <= 1024 else pltpu.VMEM((1, det, panel), jnp.bfloat16)
    return pl.pallas_call(
        functools.partial(gram_kernel, src, dets, touch, max(1, min(src, 32 // src)), 16),
        out_shape=[jax.ShapeDtypeStruct((det, panel), jnp.float32)] * 2,
        in_specs=[pl.BlockSpec(memory_space=pltpu.SMEM)] + [vmem] * 6,
        out_specs=[vmem] * 2,
        scratch_shapes=[
            pltpu.VMEM((edge, touch * det, edge), jnp.bfloat16),
            pltpu.VMEM((edge * 16, edge), jnp.float32),
            pltpu.VMEM((src, share, touch * det, edge), jnp.bfloat16),
            pltpu.VMEM((src, share // 2, touch * det, edge), jnp.bfloat16),
            block, second, block, block, block, line, line,
            dma((src,)), dma((src,)), dma((src,)), dma((src,)),
            dma((3, src)), dma((3, src)), dma((2,)),
        ],
        compiler_params=pltpu.CompilerParams(
            collective_id=0, has_side_effects=True, vmem_limit_bytes=60 << 20
        ),
        cost_estimate=pl.CostEstimate(
            flops=8 * panel * panel * share * edge * 2,
            bytes_accessed=4 * det * touch * edge * edge,
            transcendentals=0,
        ),
    )(owners, patches, bands, panel_own, panel_own.T, other_own, other_own.T)


def solution(mesh):
    return jax.shard_map(
        on_device,
        mesh=mesh,
        in_specs=(
            P(("det", "src"), None, None, None),
            P(("det", "src"), None),
            P("src", None, None),
        ),
        out_specs=(P(("det", "src"), None), P(("det", "src"), None)),
        check_vma=False,
    )
```

```python
import functools

import jax
import jax.numpy as jnp
from jax import lax
from jax.experimental import pallas as pl
from jax.experimental.pallas import tpu as pltpu
from jax.sharding import PartitionSpec as P

MESH = pl.DeviceIdType.MESH


def make_bands(taps, edge):
    count = taps.shape[-1]
    place = jnp.arange(edge, dtype=jnp.int32)
    offset = place[None, :] - place[:, None] + count // 2
    table = (offset[None] == jnp.arange(count, dtype=jnp.int32)[:, None, None]).astype(jnp.float32)
    return jnp.einsum("...t,tij->...ij", taps, table, precision=lax.Precision.HIGHEST).astype(
        jnp.bfloat16
    )


def spread_kernel(
    src, dets, own_ref, tap_ref, mine_ref, other_ref, taps_ref,
    mine, other, taps, m_send, m_recv, o_send, o_recv, t_send, t_recv,
):
    me, pd = lax.axis_index("src"), lax.axis_index("det")
    partner = lax.rem(pd + dets // 2, dets)
    barrier = pltpu.get_barrier_semaphore()

    @pl.loop(1, src)
    def _(o):
        to = lax.rem(me + o, src)
        pl.semaphore_signal(barrier, inc=1, device_id=(pd, to), device_id_type=MESH)

    @pl.loop(0, src)
    def _(o):
        to = lax.rem(me + o, src)
        pl.semaphore_signal(barrier, inc=1, device_id=(partner, to), device_id_type=MESH)

    pl.semaphore_wait(barrier, 2 * src - 1)

    def copy(o, source, target, send, recv, panel):
        return pltpu.make_async_remote_copy(
            src_ref=source,
            dst_ref=target.at[me],
            send_sem=send.at[o],
            recv_sem=recv.at[o],
            device_id=(panel, lax.rem(me + o, src)),
            device_id_type=MESH,
        )

    @pl.loop(1, src)
    def _(o):
        copy(o, tap_ref, taps, t_send, t_recv, pd).start()
        copy(o, own_ref, mine, m_send, m_recv, pd).start()

    @pl.loop(0, src)
    def _(o):
        copy(o, own_ref, other, o_send, o_recv, partner).start()

    taps[me] = tap_ref[...]
    mine[me] = own_ref[...]

    @pl.loop(1, src)
    def _(o):
        copy(o, tap_ref, taps, t_send, t_recv, pd).wait()
        copy(o, own_ref, mine, m_send, m_recv, pd).wait()

    @pl.loop(0, src)
    def _(o):
        copy(o, own_ref, other, o_send, o_recv, partner).wait()

    taps_ref[...] = taps[...]
    mine_ref[...] = mine[...]
    other_ref[...] = other[...]


def spread(owners, tap_weights, src, dets):
    vmem = pl.BlockSpec(memory_space=pltpu.VMEM)
    own = (src, *owners.shape)
    tap = (src, *tap_weights.shape)
    return pl.pallas_call(
        functools.partial(spread_kernel, src, dets),
        out_shape=[
            jax.ShapeDtypeStruct(own, jnp.int32),
            jax.ShapeDtypeStruct(own, jnp.int32),
            jax.ShapeDtypeStruct(tap, jnp.float32),
        ],
        in_specs=[vmem] * 2,
        out_specs=[vmem] * 3,
        scratch_shapes=[
            pltpu.VMEM(own, jnp.int32), pltpu.VMEM(own, jnp.int32), pltpu.VMEM(tap, jnp.float32),
        ] + [pltpu.SemaphoreType.DMA((src,))] * 6,
        compiler_params=pltpu.CompilerParams(
            collective_id=1, has_side_effects=True, vmem_limit_bytes=16 << 20
        ),
    )(owners, tap_weights)


def gram_kernel(
    src, dets, touch, group, step,
    owner_ref, patch_ref, band_ref, po_ref, pot_ref, oo_ref, oot_ref,
    self_ref, cross_ref,
    s_ref, spread_ref, mine, theirs, out_a, out_b, in_self, in_row, in_col, col_out, col_in,
    x_send, x_recv, m_send, m_recv, g_send, g_recv, c_sem,
):
    me, pd = lax.axis_index("src"), lax.axis_index("det")
    partner = lax.rem(pd + dets // 2, dets)
    upper, other_upper = pd // (dets // 2), partner // (dets // 2)
    share = mine.shape[1]
    half = share // 2
    det = mine.shape[2] // touch
    panel = src * det

    barrier = pltpu.get_barrier_semaphore()

    @pl.loop(1, src)
    def _(o):
        to = lax.rem(me + o, src)
        pl.semaphore_signal(barrier, inc=1, device_id=(pd, to), device_id_type=MESH)

    @pl.loop(0, src)
    def _(o):
        to = lax.rem(me + o, src)
        pl.semaphore_signal(barrier, inc=1, device_id=(partner, to), device_id_type=MESH)

    pl.semaphore_wait(barrier, 2 * src - 1)

    def cross_copy(o, first=0, count=touch * det):
        to = lax.rem(me + o, src)
        records = pl.ds(first, count)
        return pltpu.make_async_remote_copy(
            src_ref=s_ref.at[pl.ds(to * share + other_upper * half, half), records],
            dst_ref=theirs.at[me, :, records],
            send_sem=x_send.at[o],
            recv_sem=x_recv.at[o],
            device_id=(partner, to),
            device_id_type=MESH,
        )

    def self_copy(o, first=0, count=touch * det):
        to = lax.rem(me + o, src)
        records = pl.ds(first, count)
        return pltpu.make_async_remote_copy(
            src_ref=s_ref.at[pl.ds(to * share, share), records],
            dst_ref=mine.at[me, :, records],
            send_sem=m_send.at[o],
            recv_sem=m_recv.at[o],
            device_id=(pd, to),
            device_id_type=MESH,
        )

    def gram_copy(kind, o, source, target):
        to = lax.rem(me + o, src)
        return pltpu.make_async_remote_copy(
            src_ref=source.at[to],
            dst_ref=target.at[me],
            send_sem=g_send.at[kind, o],
            recv_sem=g_recv.at[kind, o],
            device_id=(pd, to),
            device_id_type=MESH,
        )

    def piece(ref, start, count, first, depth, t):
        return jnp.concatenate(
            [
                ref[pl.ds(start, count), first + k, t * det : (t + 1) * det, :].reshape(
                    count * det, ref.shape[3]
                )
                for k in range(depth)
            ],
            axis=1,
        )

    def partial(left, left_at, left_own, right, right_at, right_own, depth, out):
        @pl.loop(0, src // group)
        def _(g):
            start = pl.multiple_of(g * (group * det), group * det)
            total = None
            for u in range(touch):
                wide = piece(right, 0, src, right_at, depth, u)
                for t in range(touch):
                    part = lax.dot_general(
                        piece(left, g * group, group, left_at, depth, t),
                        wide,
                        (((1,), (1,)), ((), ())),
                        preferred_element_type=jnp.float32,
                    )
                    same = (
                        left_own[pl.ds(start, group * det), t : t + 1] == right_own[u : u + 1, :]
                    )
                    part = jnp.where(same, part, 0.0)
                    total = part if total is None else total + part
            out[pl.ds(g * group, group)] = total.reshape(group, det, panel).astype(jnp.bfloat16)

    def scatter(kind, source, target):
        @pl.loop(1, src)
        def _(o):
            gram_copy(kind, o, source, target).start()

        target[me] = source[me]

    def collect(kind, source, target):
        @pl.loop(1, src)
        def _(o):
            gram_copy(kind, o, source, target).wait_recv()

        total = target[0].astype(jnp.float32)
        for i in range(1, src):
            total = total + target[i].astype(jnp.float32)
        return total

    def sent(kind, source, target):
        @pl.loop(1, src)
        def _(o):
            gram_copy(kind, o, source, target).wait_send()

    edge = patch_ref.shape[2]
    steps = det // step

    @pl.loop(0, touch * steps)
    def _(q):
        t, base = q // steps, lax.rem(q, steps) * step
        for i in range(step):
            named = owner_ref[base + i, t]
            middle = lax.dot_general(
                patch_ref[base + i, t],
                band_ref[named, 0],
                (((1,), (1,)), ((), ())),
                preferred_element_type=jnp.float32,
            ).astype(jnp.bfloat16)
            spread_ref[pl.ds(i, edge, stride=step), :] = jnp.dot(
                band_ref[named, 1], middle, preferred_element_type=jnp.float32
            )
        first = pl.multiple_of(q * step, step)
        s_ref[:, pl.ds(first, step), :] = (
            spread_ref[...].reshape(edge, step, edge).astype(jnp.bfloat16)
        )

        @pl.loop(0, src)
        def _(o):
            cross_copy(o, first, step).start()

        @pl.when(lax.rem(q, steps) == steps - 1)
        def _():
            @pl.loop(1, src)
            def _(o):
                self_copy(o, pl.multiple_of(t * det, det), det).start()

    own = pltpu.make_async_copy(s_ref.at[pl.ds(me * share, share)], mine.at[me], m_send.at[0])
    own.start()
    own.wait()

    @pl.loop(1, src)
    def _(o):
        self_copy(o).wait()

    partial(mine, 0, po_ref, mine, 0, pot_ref, share, out_a)
    scatter(0, out_a, in_self)
    self_ref[...] = collect(0, out_a, in_self)
    sent(0, out_a, in_self)

    @pl.loop(0, src)
    def _(o):
        cross_copy(o).wait()

    partial(theirs, 0, oo_ref, mine, upper * half, pot_ref, half, out_a)
    scatter(1, out_a, in_col)
    single = out_b.shape[0] < src
    if single:
        sent(1, out_a, in_col)
        out_b = out_a
    partial(mine, upper * half, po_ref, theirs, 0, oot_ref, half, out_b)
    scatter(2, out_b, in_row)
    col_out[...] = collect(1, out_a, in_col).astype(jnp.bfloat16)
    last = pltpu.make_async_remote_copy(
        src_ref=col_out,
        dst_ref=col_in,
        send_sem=c_sem.at[0],
        recv_sem=c_sem.at[1],
        device_id=(partner, me),
        device_id_type=MESH,
    )
    last.start()
    rows = collect(2, out_b, in_row)
    if not single:
        sent(1, out_a, in_col)
    sent(2, out_b, in_row)
    last.wait()
    cross_ref[...] = rows + col_in[...].astype(jnp.float32)


def on_device(patches, owners, tap_weights):
    src = lax.axis_size("src")
    dets = lax.axis_size("det")
    det, touch, edge, _ = patches.shape
    panel = det * src
    share = edge // src
    panel_own, other_own, taps = spread(owners.T, tap_weights, src, dets)
    panel_own = panel_own.transpose(1, 0, 2).reshape(touch, panel)
    other_own = other_own.transpose(1, 0, 2).reshape(touch, panel)
    bands = make_bands(taps.reshape(src, 2, -1), edge)
    vmem = pl.BlockSpec(memory_space=pltpu.VMEM)
    dma = pltpu.SemaphoreType.DMA
    block = pltpu.VMEM((src, det, panel), jnp.bfloat16)
    line = pltpu.VMEM((det, panel), jnp.bfloat16)
    second = block if panel <= 1024 else pltpu.VMEM((1, det, panel), jnp.bfloat16)
    return pl.pallas_call(
        functools.partial(gram_kernel, src, dets, touch, max(1, min(src, 32 // src)), 16),
        out_shape=[jax.ShapeDtypeStruct((det, panel), jnp.float32)] * 2,
        in_specs=[pl.BlockSpec(memory_space=pltpu.SMEM)] + [vmem] * 6,
        out_specs=[vmem] * 2,
        scratch_shapes=[
            pltpu.VMEM((edge, touch * det, edge), jnp.bfloat16),
            pltpu.VMEM((edge * 16, edge), jnp.float32),
            pltpu.VMEM((src, share, touch * det, edge), jnp.bfloat16),
            pltpu.VMEM((src, share // 2, touch * det, edge), jnp.bfloat16),
            block, second, block, block, block, line, line,
            dma((src,)), dma((src,)), dma((src,)), dma((src,)),
            dma((3, src)), dma((3, src)), dma((2,)),
        ],
        compiler_params=pltpu.CompilerParams(
            collective_id=0, has_side_effects=True, vmem_limit_bytes=60 << 20
        ),
        cost_estimate=pl.CostEstimate(
            flops=8 * panel * panel * share * edge * 2,
            bytes_accessed=4 * det * touch * edge * edge,
            transcendentals=0,
        ),
    )(owners, patches, bands, panel_own.T, panel_own, other_own.T, other_own)


def solution(mesh):
    return jax.shard_map(
        on_device,
        mesh=mesh,
        in_specs=(
            P(("det", "src"), None, None, None),
            P(("det", "src"), None),
            P("src", None, None),
        ),
        out_specs=(P(("det", "src"), None), P(("det", "src"), None)),
        check_vma=False,
    )
```
